32 devices in a mesh: groups: 2 (over y), lat: 4 (over z), wid: 2 (over x), dat: 2 (over core).
Axes of the slice: x: 2, y: 2, z: 4, core: 2. Of those that a mesh axis runs over, the one named last changes fastest.
Arguments:
- inputs: bfloat16 [1024, 3584], P(('groups', 'dat'), 'wid'), parts along dimension 0, may hold values from -6 to 6
- weight: bfloat16 [16384, 3584], P(('groups', 'lat', 'dat'), 'wid'), parts along dimension 0, may hold values from -0.09375 to 0.09375
- enc_bias: float32 [16384], P(('groups', 'lat')), parts along dimension 0, may hold values from -3 to 3
- dec_bias: float32 [7168], P(('groups', 'wid')), parts along dimension 0, may hold values from -5 to 5
- row_code: int32 [1024], P('groups'), parts along dimension 0, may hold values from 1 to 4092
- lat_code: int32 [16384], P(('groups', 'lat')), parts along dimension 0, may hold values from 1 to 4092
- lat_thr: int32 [16384], P(('groups', 'lat')), parts along dimension 0, may hold values from 41 to 204
- loss_scale: float32 [1], replicated, may hold values from 8 to 32
Outputs:
- grad_weight: bfloat16 [16384, 3584], P(('groups', 'lat', 'dat'), 'wid'), parts along dimension 0
- grad_enc_bias: float32 [16384], P(('groups', 'lat')), parts along dimension 0
- grad_dec_bias: float32 [7168], P(('groups', 'wid')), parts along dimension 0
The draws below stay inside these ranges and needn't reach their ends.
There are 2 independent parts, one for each index of `groups`. The reference program is written for one: setup_inputs(seed, part) draws one part's arguments, and reference() takes and returns one part's arrays. A program takes and returns all parts, laid end to end along the dimension named above; an argument that names none is the same for every part. Nothing has to cross between parts.
All inputs are finite; a program needn't handle non-finite values.
Results may differ from the reference program's by a relative error of at most 0.017.
Values may be sent and summed in bfloat16 or wider, within the bound.
A program may use at most 128 MiB of HBM per device.

```python
import jax
import jax.numpy as jnp
from jax import lax

D = 3584
TOK_DEV = 256
L = 8192
TOKENS = 512
N_WID = 2
N_DAT = 2


def with_ends(drawn, key, smallest, high):
    shape = drawn.shape
    index_at = [jax.random.randint(jax.random.fold_in(key, axis), (), 0, shape[axis]) for axis in range(len(shape))]
    drawn = drawn.at[tuple(index_at)].set(smallest)
    longest = shape.index(max(shape))
    index_at[longest] = (index_at[longest] + 1) % shape[longest]
    return drawn.at[tuple(index_at)].set(high)


def shard_levels(key, shape, shards, low, top_value):
    def one(dim, blocks):
        heights = jax.random.uniform(jax.random.fold_in(jax.random.fold_in(key, 6), dim), (blocks,), jnp.float32, low / len(shards), top_value / len(shards))
        return jnp.repeat(jnp.exp(heights), shape[dim] // blocks).reshape((-1,) + (1,) * (len(shape) - dim - 1))

    loudness = one(*shards[0])
    for cut in shards[1:]:
        loudness = loudness * one(*cut)
    return loudness


def bell_draw(key, extent, scale, reach, split=(), kind=jnp.bfloat16):
    factor_of = shard_levels(key, extent, split, -0.22, 0.18) if split else 1.0
    drawn = jax.random.normal(key, extent, jnp.float32) * scale * factor_of
    return jnp.minimum(jnp.maximum(drawn, -reach), reach).astype(kind)


def setup_inputs(seed: int = 0, part: int = 0) -> dict:
    streams_of = jax.random.split(jax.random.key(seed), 9)
    part_splits = jax.random.split(jax.random.fold_in(streams_of[8], part), 9)
    return {
        "inputs": bell_draw(part_splits[0], (TOKENS, D), 1.0, 6.0, ((0, 2), (1, 2))),
        "weight": bell_draw(part_splits[1], (L, D), D ** -0.5, 0.09375, ((0, 8), (1, 2))),
        "enc_bias": bell_draw(part_splits[2], (L,), 0.5, 3.0, ((0, 4),), jnp.float32),
        "dec_bias": bell_draw(part_splits[3], (D,), 1.0, 5.0, ((0, 2),), jnp.float32),
        "row_code": with_ends(jax.random.randint(part_splits[4], (TOKENS,), 1, 4093), jax.random.fold_in(part_splits[4], 1), 1, 4092).astype(jnp.int32),
        "lat_code": with_ends(jax.random.randint(part_splits[5], (L,), 1, 4093), jax.random.fold_in(part_splits[5], 1), 1, 4092).astype(jnp.int32),
        "lat_thr": with_ends(jax.random.randint(part_splits[6], (L,), 41, 205), jax.random.fold_in(part_splits[6], 1), 41, 204).astype(jnp.int32),
        "loss_scale": jnp.clip(jax.random.uniform(streams_of[7], (1,), jnp.float32, 8.0, 32.0), 8.0, 32.0),
    }


def block_sum(left, weight):
    width_blk = D // N_WID
    total = jnp.zeros((left.shape[0], weight.shape[0]), jnp.float32)
    for block in range(N_WID):
        lo = block * width_blk
        part = jnp.dot(left[:, lo:lo + width_blk], weight[:, lo:lo + width_blk].T, preferred_element_type=jnp.float32)
        rounded = lax.optimization_barrier(part.astype(jnp.bfloat16))
        total = total + rounded.astype(jnp.float32)
    return total


def reference(inputs, weight, enc_bias, dec_bias, row_code, lat_code, lat_thr, loss_scale):
    active = ((row_code[:, None] * lat_code[None, :]) % 4093) < lat_thr[None, :]
    pre = block_sum(inputs, weight) + enc_bias[None, :]
    acts = jnp.where(active, pre, 0.0).astype(jnp.bfloat16)
    recon = jnp.dot(acts, weight, preferred_element_type=jnp.float32) + dec_bias[None, :]
    g_rec = loss_scale[0] * (2.0 / TOKENS) * (recon - inputs.astype(jnp.float32))
    g_bf = g_rec.astype(jnp.bfloat16)
    g_acts = block_sum(g_bf, weight)
    g_pre = jnp.where(active, g_acts, 0.0).astype(jnp.bfloat16)
    grad_total = jnp.zeros(weight.shape, jnp.float32)
    for block in range(N_DAT):
        lo = block * TOK_DEV
        term = jnp.dot(acts[lo:lo + TOK_DEV].T, g_bf[lo:lo + TOK_DEV], preferred_element_type=jnp.float32)
        term = term + jnp.dot(g_pre[lo:lo + TOK_DEV].T, inputs[lo:lo + TOK_DEV], preferred_element_type=jnp.float32)
        rounded = lax.optimization_barrier(term.astype(jnp.bfloat16))
        grad_total = grad_total + rounded.astype(jnp.float32)
    grad_weight = grad_total.astype(jnp.bfloat16)
    grad_enc_bias = jnp.sum(g_pre.astype(jnp.float32), axis=0)
    grad_dec_bias = jnp.sum(g_rec, axis=0)
    return (grad_weight, grad_enc_bias, grad_dec_bias)
```

```python
import jax
import jax.numpy as jnp
from jax import lax
from jax.sharding import PartitionSpec as P


def times_rows(left, right):
    return lax.dot_general(
        left, right, (((1,), (1,)), ((), ())), preferred_element_type=jnp.float32
    )


def columns_first(left, right):
    return lax.dot_general(
        left, right, (((0,), (0,)), ((), ())), preferred_element_type=jnp.float32
    )


def per_device(inputs, weight, enc_bias, dec_bias, row_code, lat_code, lat_thr, loss_scale):
    place = lax.axis_index("dat")
    lats = weight.shape[0]
    mine = lambda v: lax.dynamic_slice_in_dim(v, place * lats, lats, 0)
    rows = lax.all_gather(inputs, "dat", axis=0, tiled=True)
    total_rows = rows.shape[0]
    active = row_code[:, None] * mine(lat_code)[None, :] % 4093 < mine(lat_thr)[None, :]
    pre = (
        lax.psum(times_rows(rows, weight).astype(jnp.bfloat16), "wid").astype(jnp.float32)
        + mine(enc_bias)[None, :]
    )
    acts = jnp.where(active, pre, 0.0).astype(jnp.bfloat16)
    partial_value = jnp.dot(acts, weight, preferred_element_type=jnp.float32)
    recon = lax.psum(partial_value.astype(jnp.bfloat16), ("lat", "dat")).astype(jnp.float32)
    recon = recon + dec_bias[None, :]
    g_rec = loss_scale[0] * (2.0 / total_rows) * (recon - rows.astype(jnp.float32))
    g_bf = g_rec.astype(jnp.bfloat16)
    g_acts = lax.psum(times_rows(g_bf, weight).astype(jnp.bfloat16), "wid").astype(jnp.float32)
    g_pre = jnp.where(active, g_acts, 0.0).astype(jnp.bfloat16)
    grad_weight = (columns_first(acts, g_bf) + columns_first(g_pre, rows)).astype(jnp.bfloat16)
    latent_total = jnp.sum(g_pre.astype(jnp.float32), axis=0)
    grad_enc_bias = lax.all_gather(latent_total, "dat", axis=0, tiled=True)
    return (grad_weight, grad_enc_bias, jnp.sum(g_rec, axis=0))


def solution(mesh):
    return jax.shard_map(
        per_device,
        mesh=mesh,
        in_specs=(
            P(("groups", "dat"), "wid"),
            P(("groups", "lat", "dat"), "wid"),
            P(("groups", "lat")),
            P(("groups", "wid")),
            P("groups"),
            P(("groups", "lat")),
            P(("groups", "lat")),
            P(),
        ),
        out_specs=(P(("groups", "lat", "dat"), "wid"), P(("groups", "lat")), P(("groups", "wid"))),
        check_vma=False,
    )
```

```python
import functools

import jax
import jax.numpy as jnp
from jax import lax
from jax.experimental import pallas as pl
from jax.experimental.pallas import tpu as pltpu
from jax.sharding import PartitionSpec as P

MESH = pl.DeviceIdType.MESH
BF16 = jnp.bfloat16
F32 = jnp.float32
CHUNKS = 4
TILE = 256
STAGE_AT = (0, 10, 15, 22, 29, 32, 40)
CHUNK_STEP = 8


def times_rows(left, right):
    return lax.dot_general(
        left, right, (((1,), (1,)), ((), ())), preferred_element_type=jnp.float32
    )


def columns_first(left, right):
    return lax.dot_general(
        left, right, (((0,), (0,)), ((), ())), preferred_element_type=jnp.float32
    )


def per_device(inputs, weight, enc_bias, dec_bias, row_code, lat_code, lat_thr, loss_scale):
    place = lax.axis_index("dat")
    lats = weight.shape[0]
    mine = lambda v: lax.dynamic_slice_in_dim(v, place * lats, lats, 0)
    rows = lax.all_gather(inputs, "dat", axis=0, tiled=True)
    total_rows = rows.shape[0]
    active = row_code[:, None] * mine(lat_code)[None, :] % 4093 < mine(lat_thr)[None, :]
    pre = (
        lax.psum(times_rows(rows, weight).astype(jnp.bfloat16), "wid").astype(jnp.float32)
        + mine(enc_bias)[None, :]
    )
    acts = jnp.where(active, pre, 0.0).astype(jnp.bfloat16)
    partial_value = jnp.dot(acts, weight, preferred_element_type=jnp.float32)
    recon = lax.psum(partial_value.astype(jnp.bfloat16), ("lat", "dat")).astype(jnp.float32)
    recon = recon + dec_bias[None, :]
    g_rec = loss_scale[0] * (2.0 / total_rows) * (recon - rows.astype(jnp.float32))
    g_bf = g_rec.astype(jnp.bfloat16)
    g_acts = lax.psum(times_rows(g_bf, weight).astype(jnp.bfloat16), "wid").astype(jnp.float32)
    g_pre = jnp.where(active, g_acts, 0.0).astype(jnp.bfloat16)
    grad_weight = (columns_first(acts, g_bf) + columns_first(g_pre, rows)).astype(jnp.bfloat16)
    latent_total = jnp.sum(g_pre.astype(jnp.float32), axis=0)
    grad_enc_bias = lax.all_gather(latent_total, "dat", axis=0, tiled=True)
    return (grad_weight, grad_enc_bias, jnp.sum(g_rec, axis=0))


def kernel(
    n_wid, n_lat, scale_ref, x_ref, w_ref, eb_ref, db_ref, rc_ref, lc_ref, thr_ref,
    gw_ref, ge_ref, gd_ref,
    x_all, p_out, p_in, acts_t, rec, rec_in, summed, pieces, g_all, q_out, q_in, g_pre_t, grad, eb_sum,
    x_sem, p_sem, c_sem, s_sem, a_sem, h_sem, q_sem, e_sem,
):
    wid, lat, dat = lax.axis_index("wid"), lax.axis_index("lat"), lax.axis_index("dat")
    other = 1 - dat
    half, width = x_all.shape[2:]
    lats = w_ref.shape[0]
    rows = 2 * half
    wid_peers = [lax.rem(wid + k, n_wid) for k in range(1, n_wid)]
    lat_peers = [lax.rem(lat + k, n_lat) for k in range(1, n_lat)]

    barrier = pltpu.get_barrier_semaphore()
    everyone = [{"dat": other}] + [{"wid": p} for p in wid_peers] + [{"lat": p} for p in lat_peers]
    for peer in everyone:
        pl.semaphore_signal(barrier, inc=1, device_id=peer, device_id_type=MESH)
    pl.semaphore_wait(barrier, len(everyone))

    def copy(src, dst, sems, peer):
        return pltpu.make_async_remote_copy(
            src_ref=src, dst_ref=dst, send_sem=sems.at[0], recv_sem=sems.at[1],
            device_id=peer, device_id_type=MESH,
        )

    def x_copy(c):
        return copy(x_ref.at[c], x_all.at[c, dat], x_sem.at[c], {"dat": other})

    def p_copies(c):
        return [copy(p_out.at[c], p_in.at[c, k], p_sem.at[c, k], {"wid": p}) for k, p in enumerate(wid_peers)]

    def q_copies(c):
        return [copy(q_out.at[c], q_in.at[c, k], q_sem.at[c, k], {"wid": p}) for k, p in enumerate(wid_peers)]

    def c_copy(c):
        return copy(rec.at[c, other], rec_in.at[c], c_sem.at[c], {"dat": other})

    def s_copies(c):
        return [copy(summed.at[c, p], pieces.at[c, k], s_sem.at[c, k], {"lat": p}) for k, p in enumerate(lat_peers)]

    def a_copies(c):
        return [
            copy(g_all.at[c, dat, lat], g_all.at[c, dat, lat], a_sem.at[c, k], {"lat": p})
            for k, p in enumerate(lat_peers)
        ]

    def h_copy(c):
        return copy(g_all.at[c, dat], g_all.at[c, dat], h_sem.at[c], {"dat": other})

    def active(c):
        product = rc_ref[c].astype(F32) * lc_ref[dat].astype(F32)
        left = product - jnp.floor(product * (1.0 / 4093.0)) * 4093.0
        left = jnp.where(left < 0.0, left + 4093.0, left)
        left = jnp.where(left >= 4093.0, left - 4093.0, left)
        return left < thr_ref[dat].astype(F32)

    def by_latents(value, out, c):
        for t in range(lats // TILE):
            cols = slice(t * TILE, (t + 1) * TILE)
            out[c, :, cols] = times_rows(value, w_ref[cols, :]).astype(BF16)

    def total(out, into, c):
        value = out[c].astype(F32)
        for k in range(n_wid - 1):
            value = value + into[c, k].astype(F32)
        return value

    def encode(c):
        x_copy(c).wait()
        by_latents(x_all[c].reshape(rows, width), p_out, c)
        for one in p_copies(c):
            one.start()

    def decode(c):
        for one in p_copies(c):
            one.wait()
        acts = jnp.where(active(c), total(p_out, p_in, c) + eb_ref[dat], 0.0)
        acts_t[:, c * rows:(c + 1) * rows] = acts.T.astype(BF16)
        acts = acts.astype(BF16)
        for t in range(width // TILE):
            cols = slice(t * TILE, (t + 1) * TILE)
            part = jnp.dot(acts, w_ref[:, cols], preferred_element_type=F32)
            rec[c, :, :, cols] = part.astype(BF16).reshape(2, half, TILE)
        c_copy(c).start()

    def core_sum(c):
        c_copy(c).wait()
        both = rec[c, dat].astype(F32) + rec_in[c].astype(F32)
        summed[c] = both.astype(BF16).reshape(summed.shape[1:])
        for one in s_copies(c):
            one.start()

    def gradient(c):
        for one in s_copies(c):
            one.wait()
        recon = summed[c, lat].astype(F32)
        for k in range(n_lat - 1):
            recon = recon + pieces[c, k].astype(F32)
        own = x_piece(c)
        g_rec = scale_ref[0] * (2.0 / (rows * CHUNKS)) * (recon + db_ref[...] - own.astype(F32))
        g_all[c, dat, lat] = g_rec.astype(BF16)
        for one in a_copies(c):
            one.start()

    def x_piece(c):
        count = half // n_lat
        return x_ref[c, pl.ds(pl.multiple_of(lat * count, count), count), :]

    def share(c):
        for one in a_copies(c):
            one.wait()
        h_copy(c).start()

    def back(c):
        h_copy(c).wait()
        g_rows = g_all[c].reshape(rows, width)
        column = jnp.sum(g_rows.astype(F32), axis=0, keepdims=True)
        gd_ref[...] = column if c == 0 else gd_ref[...] + column
        by_latents(g_rows, q_out, c)
        for one in q_copies(c):
            one.start()

    def gate(c):
        for one in q_copies(c):
            one.wait()
        g_pre = jnp.where(active(c), total(q_out, q_in, c), 0.0).astype(BF16).astype(F32)
        g_pre_t[:, c * rows:(c + 1) * rows] = g_pre.T.astype(BF16)
        column = jnp.sum(g_pre, axis=0, keepdims=True)
        eb_sum[dat] = column if c == 0 else eb_sum[dat] + column

    for c in range(CHUNKS):
        x_copy(c).start()
    x_all[:, dat] = x_ref[...]
    stages = (encode, decode, core_sum, gradient, share, back, gate)
    order = sorted(
        (STAGE_AT[s] + (CHUNK_STEP if s else 1) * c, s, c) for s in range(len(stages)) for c in range(CHUNKS)
    )
    for _, s, c in order:
        if s == len(stages) - 1 and c == CHUNKS - 1:
            for t in range(width // TILE):
                cols = slice(t * TILE, (t + 1) * TILE)
                right = g_all[:, :, :, :, cols].reshape(CHUNKS * rows, TILE)
                grad[:, cols] = jnp.dot(acts_t[...], right, preferred_element_type=F32)
        stages[s](c)
    e_copy = copy(eb_sum.at[dat], eb_sum.at[dat], e_sem, {"dat": other})
    e_copy.start()
    for t in range(width // TILE):
        cols = slice(t * TILE, (t + 1) * TILE)
        right = x_all[:, :, :, cols].reshape(CHUNKS * rows, TILE)
        grown = grad[:, cols] + jnp.dot(g_pre_t[...], right, preferred_element_type=F32)
        gw_ref[:, cols] = grown.astype(BF16)
    e_copy.wait()
    ge_ref[...] = eb_sum[...]


def fused(n_wid, n_lat, inputs, weight, enc_bias, dec_bias, row_code, lat_code, lat_thr, loss_scale):
    lats, width = weight.shape
    half = inputs.shape[0] // CHUNKS
    rows, piece = 2 * half, half // n_lat
    whole = pl.BlockSpec(memory_space=pltpu.VMEM)
    codes = jnp.swapaxes(row_code.reshape(2, CHUNKS, half), 0, 1).reshape(CHUNKS, rows, 1)
    pair = lambda v: v.reshape(2, 1, lats)
    sems = lambda *shape: pltpu.SemaphoreType.DMA(shape + (2,))
    grad_weight, grad_enc_bias, grad_dec_bias = pl.pallas_call(
        functools.partial(kernel, n_wid, n_lat),
        out_shape=(
            jax.ShapeDtypeStruct((lats, width), BF16),
            jax.ShapeDtypeStruct((2, 1, lats), F32),
            jax.ShapeDtypeStruct((1, width), F32),
        ),
        in_specs=[pl.BlockSpec(memory_space=pltpu.SMEM)] + [whole] * 7,
        out_specs=(whole,) * 3,
        scratch_shapes=[
            pltpu.VMEM((CHUNKS, 2, half, width), BF16),
            pltpu.VMEM((CHUNKS, rows, lats), BF16),
            pltpu.VMEM((CHUNKS, n_wid - 1, rows, lats), BF16),
            pltpu.VMEM((lats, CHUNKS * rows), BF16),
            pltpu.VMEM((CHUNKS, 2, half, width), BF16),
            pltpu.VMEM((CHUNKS, half, width), BF16),
            pltpu.VMEM((CHUNKS, n_lat, piece, width), BF16),
            pltpu.VMEM((CHUNKS, n_lat - 1, piece, width), BF16),
            pltpu.VMEM((CHUNKS, 2, n_lat, piece, width), BF16),
            pltpu.VMEM((CHUNKS, rows, lats), BF16),
            pltpu.VMEM((CHUNKS, n_wid - 1, rows, lats), BF16),
            pltpu.VMEM((lats, CHUNKS * rows), BF16),
            pltpu.VMEM((lats, width), F32),
            pltpu.VMEM((2, 1, lats), F32),
            sems(CHUNKS), sems(CHUNKS, n_wid - 1), sems(CHUNKS), sems(CHUNKS, n_lat - 1),
            sems(CHUNKS, n_lat - 1), sems(CHUNKS), sems(CHUNKS, n_wid - 1), sems(),
        ],
        compiler_params=pltpu.CompilerParams(
            collective_id=0, has_side_effects=True, vmem_limit_bytes=56 * 1024 * 1024
        ),
    )(
        loss_scale, inputs.reshape(CHUNKS, half, width), weight, pair(enc_bias),
        dec_bias.reshape(1, width), codes, pair(lat_code), pair(lat_thr),
    )
    return (grad_weight, grad_enc_bias.reshape(-1), grad_dec_bias.reshape(-1))


def fits(mesh, rows, lats, width):
    n_wid, n_lat = mesh.shape["wid"], mesh.shape["lat"]
    return (
        mesh.shape["dat"] == 2 and n_wid == 2 and 2 <= n_lat <= 8
        and rows % (CHUNKS * n_lat * 16) == 0 and lats % TILE == 0 and width % TILE == 0
        and lats * width <= 2 ** 21 and rows <= 256
    )


def solution(mesh):
    def body(inputs, weight, *rest):
        if fits(mesh, inputs.shape[0], weight.shape[0], weight.shape[1]):
            return fused(mesh.shape["wid"], mesh.shape["lat"], inputs, weight, *rest)
        return per_device(inputs, weight, *rest)

    return jax.shard_map(
        body,
        mesh=mesh,
        in_specs=(
            P(("groups", "dat"), "wid"),
            P(("groups", "lat", "dat"), "wid"),
            P(("groups", "lat")),
            P(("groups", "wid")),
            P("groups"),
            P(("groups", "lat")),
            P(("groups", "lat")),
            P(),
        ),
        out_specs=(P(("groups", "lat", "dat"), "wid"), P(("groups", "lat")), P(("groups", "wid"))),
        check_vma=False,
    )
```

```python
import functools

import jax
import jax.numpy as jnp
from jax import lax
from jax.experimental import pallas as pl
from jax.experimental.pallas import tpu as pltpu
from jax.sharding import PartitionSpec as P

MESH = pl.DeviceIdType.MESH
BF16 = jnp.bfloat16
F32 = jnp.float32
CHUNKS = 4
TILE = 256
LANES = 128
STAGE_AT = (0, 10, 15, 30, 45, 48, 60)
CHUNK_STEP = 10


def times_rows(left, right):
    return lax.dot_general(
        left, right, (((1,), (1,)), ((), ())), preferred_element_type=jnp.float32
    )


def columns_first(left, right):
    return lax.dot_general(
        left, right, (((0,), (0,)), ((), ())), preferred_element_type=jnp.float32
    )


def per_device(inputs, weight, enc_bias, dec_bias, row_code, lat_code, lat_thr, loss_scale):
    place = lax.axis_index("dat")
    lats = weight.shape[0]
    mine = lambda v: lax.dynamic_slice_in_dim(v, place * lats, lats, 0)
    rows = lax.all_gather(inputs, "dat", axis=0, tiled=True)
    total_rows = rows.shape[0]
    active = row_code[:, None] * mine(lat_code)[None, :] % 4093 < mine(lat_thr)[None, :]
    pre = (
        lax.psum(times_rows(rows, weight).astype(jnp.bfloat16), "wid").astype(jnp.float32)
        + mine(enc_bias)[None, :]
    )
    acts = jnp.where(active, pre, 0.0).astype(jnp.bfloat16)
    partial_value = jnp.dot(acts, weight, preferred_element_type=jnp.float32)
    recon = lax.psum(partial_value.astype(jnp.bfloat16), ("lat", "dat")).astype(jnp.float32)
    recon = recon + dec_bias[None, :]
    g_rec = loss_scale[0] * (2.0 / total_rows) * (recon - rows.astype(jnp.float32))
    g_bf = g_rec.astype(jnp.bfloat16)
    g_acts = lax.psum(times_rows(g_bf, weight).astype(jnp.bfloat16), "wid").astype(jnp.float32)
    g_pre = jnp.where(active, g_acts, 0.0).astype(jnp.bfloat16)
    grad_weight = (columns_first(acts, g_bf) + columns_first(g_pre, rows)).astype(jnp.bfloat16)
    latent_total = jnp.sum(g_pre.astype(jnp.float32), axis=0)
    grad_enc_bias = lax.all_gather(latent_total, "dat", axis=0, tiled=True)
    return (grad_weight, grad_enc_bias, jnp.sum(g_rec, axis=0))


def kernel(
    n_wid, n_lat, scale_ref, x_ref, w_ref, eb_ref, db_ref, rc_ref, lc_ref, thr_ref,
    gw_ref, ge_ref, gd_ref,
    x_all, p_out, p_in, acts_t, rec, rec_in, summed, pieces, g_all, q_out, q_in, g_pre_t, grad, done, eb_sum,
    x_sem, p_sem, c_sem, s_sem, a_sem, h_sem, q_sem, e_sem, w_sem,
):
    wid, lat, dat = lax.axis_index("wid"), lax.axis_index("lat"), lax.axis_index("dat")
    other = 1 - dat
    half, width = x_all.shape[2:]
    lats = w_ref.shape[0]
    rows = 2 * half
    wid_peers = [lax.rem(wid + k, n_wid) for k in range(1, n_wid)]
    lat_peers = [lax.rem(lat + k, n_lat) for k in range(1, n_lat)]

    barrier = pltpu.get_barrier_semaphore()
    everyone = [{"dat": other}] + [{"wid": p} for p in wid_peers] + [{"lat": p} for p in lat_peers]
    for peer in everyone:
        pl.semaphore_signal(barrier, inc=1, device_id=peer, device_id_type=MESH)
    pl.semaphore_wait(barrier, len(everyone))

    def copy(src, dst, sems, peer):
        return pltpu.make_async_remote_copy(
            src_ref=src, dst_ref=dst, send_sem=sems.at[0], recv_sem=sems.at[1],
            device_id=peer, device_id_type=MESH,
        )

    def x_copy(c):
        return copy(x_ref.at[c], x_all.at[c, dat], x_sem.at[c], {"dat": other})

    def p_copies(c):
        return [copy(p_out.at[c], p_in.at[c, k], p_sem.at[c, k], {"wid": p}) for k, p in enumerate(wid_peers)]

    def q_copies(c):
        return [copy(q_out.at[c], q_in.at[c, k], q_sem.at[c, k], {"wid": p}) for k, p in enumerate(wid_peers)]

    def c_copy(c):
        return copy(rec.at[c, other], rec_in.at[c], c_sem.at[c], {"dat": other})

    def s_copies(c):
        return [copy(summed.at[c, p], pieces.at[c, k], s_sem.at[c, k], {"lat": p}) for k, p in enumerate(lat_peers)]

    def a_copies(c):
        return [
            copy(g_all.at[c, dat, lat], g_all.at[c, dat, lat], a_sem.at[c, k], {"lat": p})
            for k, p in enumerate(lat_peers)
        ]

    def h_copy(c):
        return copy(g_all.at[c, dat], g_all.at[c, dat], h_sem.at[c], {"dat": other})

    def row_codes(c):
        line = rc_ref[...].astype(F32)
        starts = (c * half, (CHUNKS + c) * half)
        line = jnp.concatenate([line[:, at:at + half] for at in starts], axis=1)
        return jnp.broadcast_to(line, (LANES, rows)).T[:, :1]

    def active(c):
        product = row_codes(c) * lc_ref[dat].astype(F32)
        left = product - jnp.floor(product * (1.0 / 4093.0)) * 4093.0
        left = jnp.where(left < 0.0, left + 4093.0, left)
        left = jnp.where(left >= 4093.0, left - 4093.0, left)
        return left < thr_ref[dat].astype(F32)

    def by_latents(value, out, c):
        for t in range(lats // TILE):
            cols = slice(t * TILE, (t + 1) * TILE)
            out[c, :, cols] = times_rows(value, w_ref[cols, :]).astype(BF16)

    def total(out, into, c):
        value = out[c].astype(F32)
        for k in range(n_wid - 1):
            value = value + into[c, k].astype(F32)
        return value

    def encode(c):
        x_copy(c).wait()
        by_latents(x_all[c].reshape(rows, width), p_out, c)
        for one in p_copies(c):
            one.start()

    def decode(c):
        for one in p_copies(c):
            one.wait()
        acts = jnp.where(active(c), total(p_out, p_in, c) + eb_ref[dat], 0.0)
        acts_t[:, c * rows:(c + 1) * rows] = acts.T.astype(BF16)
        acts = acts.astype(BF16)
        for t in range(width // TILE):
            cols = slice(t * TILE, (t + 1) * TILE)
            part = jnp.dot(acts, w_ref[:, cols], preferred_element_type=F32)
            rec[c, :, :, cols] = part.astype(BF16).reshape(2, half, TILE)
        c_copy(c).start()

    def core_sum(c):
        c_copy(c).wait()
        both = rec[c, dat].astype(F32) + rec_in[c].astype(F32)
        summed[c] = both.astype(BF16).reshape(summed.shape[1:])
        for one in s_copies(c):
            one.start()

    def gradient(c):
        for one in s_copies(c):
            one.wait()
        recon = summed[c, lat].astype(F32)
        for k in range(n_lat - 1):
            recon = recon + pieces[c, k].astype(F32)
        own = x_piece(c)
        g_rec = scale_ref[0] * (2.0 / (rows * CHUNKS)) * (recon + bias_row() - own.astype(F32))
        g_all[c, dat, lat] = g_rec.astype(BF16)
        for one in a_copies(c):
            one.start()

    def bias_row():
        return jnp.concatenate([db_ref[i:i + 1, :] for i in range(width // LANES)], axis=1)

    def x_piece(c):
        count = half // n_lat
        return x_ref[c, pl.ds(pl.multiple_of(lat * count, count), count), :]

    def share(c):
        for one in a_copies(c):
            one.wait()
        h_copy(c).start()

    def back(c):
        h_copy(c).wait()
        g_rows = g_all[c].reshape(rows, width)
        column = jnp.sum(g_rows.astype(F32), axis=0, keepdims=True)
        for i in range(width // LANES):
            cell = column[:, i * LANES:(i + 1) * LANES]
            gd_ref[i:i + 1, :] = cell if c == 0 else gd_ref[i:i + 1, :] + cell
        by_latents(g_rows, q_out, c)
        for one in q_copies(c):
            one.start()

    def gate(c):
        for one in q_copies(c):
            one.wait()
        g_pre = jnp.where(active(c), total(q_out, q_in, c), 0.0).astype(BF16).astype(F32)
        g_pre_t[:, c * rows:(c + 1) * rows] = g_pre.T.astype(BF16)
        column = jnp.sum(g_pre, axis=0, keepdims=True)
        eb_sum[dat] = column if c == 0 else eb_sum[dat] + column

    def out_copy(t):
        cols = slice(t * TILE, (t + 1) * TILE)
        return pltpu.make_async_copy(done.at[:, cols], gw_ref.at[:, cols], w_sem.at[t])

    for c in range(CHUNKS):
        x_copy(c).start()
    x_all[:, dat] = x_ref[...]
    stages = (encode, decode, core_sum, gradient, share, back, gate)
    order = sorted(
        (STAGE_AT[s] + (CHUNK_STEP if s else 1) * c, s, c) for s in range(len(stages)) for c in range(CHUNKS)
    )
    for _, s, c in order:
        if s == len(stages) - 1 and c == CHUNKS - 1:
            for t in range(width // TILE):
                cols = slice(t * TILE, (t + 1) * TILE)
                right = g_all[:, :, :, :, cols].reshape(CHUNKS * rows, TILE)
                early = x_all[:c, :, :, cols].reshape(c * rows, TILE)
                grad[:, cols] = jnp.dot(acts_t[...], right, preferred_element_type=F32) + jnp.dot(
                    g_pre_t[:, :c * rows], early, preferred_element_type=F32
                )
        stages[s](c)
    e_copy = copy(eb_sum.at[dat], eb_sum.at[dat], e_sem, {"dat": other})
    e_copy.start()
    for t in range(width // TILE):
        cols = slice(t * TILE, (t + 1) * TILE)
        right = x_all[CHUNKS - 1, :, :, cols].reshape(rows, TILE)
        late = jnp.dot(g_pre_t[:, (CHUNKS - 1) * rows:], right, preferred_element_type=F32)
        done[:, cols] = (grad[:, cols] + late).astype(BF16)
        out_copy(t).start()
    for t in range(width // TILE):
        out_copy(t).wait()
    e_copy.wait()
    ge_ref[...] = eb_sum[...]


def fused(n_wid, n_lat, inputs, weight, enc_bias, dec_bias, row_code, lat_code, lat_thr, loss_scale):
    lats, width = weight.shape
    half = inputs.shape[0] // CHUNKS
    rows, piece = 2 * half, half // n_lat
    whole = pl.BlockSpec(memory_space=pltpu.VMEM)
    pair = lambda v: v.reshape(2, 1, lats)
    sems = lambda *shape: pltpu.SemaphoreType.DMA(shape + (2,))
    grad_weight, grad_enc_bias, grad_dec_bias = pl.pallas_call(
        functools.partial(kernel, n_wid, n_lat),
        out_shape=(
            jax.ShapeDtypeStruct((lats, width), BF16),
            jax.ShapeDtypeStruct((2, 1, lats), F32),
            jax.ShapeDtypeStruct((width // LANES, LANES), F32),
        ),
        in_specs=[pl.BlockSpec(memory_space=pltpu.SMEM)] + [whole] * 7,
        out_specs=(pl.BlockSpec(memory_space=pl.ANY), whole, whole),
        scratch_shapes=[
            pltpu.VMEM((CHUNKS, 2, half, width), BF16),
            pltpu.VMEM((CHUNKS, rows, lats), BF16),
            pltpu.VMEM((CHUNKS, n_wid - 1, rows, lats), BF16),
            pltpu.VMEM((lats, CHUNKS * rows), BF16),
            pltpu.VMEM((CHUNKS, 2, half, width), BF16),
            pltpu.VMEM((CHUNKS, half, width), BF16),
            pltpu.VMEM((CHUNKS, n_lat, piece, width), BF16),
            pltpu.VMEM((CHUNKS, n_lat - 1, piece, width), BF16),
            pltpu.VMEM((CHUNKS, 2, n_lat, piece, width), BF16),
            pltpu.VMEM((CHUNKS, rows, lats), BF16),
            pltpu.VMEM((CHUNKS, n_wid - 1, rows, lats), BF16),
            pltpu.VMEM((lats, CHUNKS * rows), BF16),
            pltpu.VMEM((lats, width), F32),
            pltpu.VMEM((lats, width), BF16),
            pltpu.VMEM((2, 1, lats), F32),
            sems(CHUNKS), sems(CHUNKS, n_wid - 1), sems(CHUNKS), sems(CHUNKS, n_lat - 1),
            sems(CHUNKS, n_lat - 1), sems(CHUNKS), sems(CHUNKS, n_wid - 1), sems(),
            pltpu.SemaphoreType.DMA((width // TILE,)),
        ],
        compiler_params=pltpu.CompilerParams(
            collective_id=0, has_side_effects=True, vmem_limit_bytes=56 * 1024 * 1024
        ),
    )(
        loss_scale, inputs.reshape(CHUNKS, half, width), weight, pair(enc_bias),
        dec_bias.reshape(width // LANES, LANES), row_code.reshape(1, -1), pair(lat_code), pair(lat_thr),
    )
    return (grad_weight, grad_enc_bias.reshape(-1), grad_dec_bias.reshape(-1))


def fits(mesh, rows, lats, width):
    n_wid, n_lat = mesh.shape["wid"], mesh.shape["lat"]
    return (
        mesh.shape["dat"] == 2 and n_wid == 2 and 2 <= n_lat <= 8
        and rows % (CHUNKS * n_lat * 16) == 0 and lats % TILE == 0 and 2 * rows % (CHUNKS * LANES) == 0 and width % TILE == 0
        and lats * width <= 2 ** 21 and rows <= 256
    )


def solution(mesh):
    def body(inputs, weight, *rest):
        if fits(mesh, inputs.shape[0], weight.shape[0], weight.shape[1]):
            return fused(mesh.shape["wid"], mesh.shape["lat"], inputs, weight, *rest)
        return per_device(inputs, weight, *rest)

    return jax.shard_map(
        body,
        mesh=mesh,
        in_specs=(
            P(("groups", "dat"), "wid"),
            P(("groups", "lat", "dat"), "wid"),
            P(("groups", "lat")),
            P(("groups", "wid")),
            P("groups"),
            P(("groups", "lat")),
            P(("groups", "lat")),
            P(),
        ),
        out_specs=(P(("groups", "lat", "dat"), "wid"), P(("groups", "lat")), P(("groups", "wid"))),
        check_vma=False,
    )
```

```python
import functools

import jax
import jax.numpy as jnp
from jax import lax
from jax.experimental import pallas as pl
from jax.experimental.pallas import tpu as pltpu
from jax.sharding import PartitionSpec as P

MESH = pl.DeviceIdType.MESH
BF16 = jnp.bfloat16
F32 = jnp.float32
CHUNKS = 4
TILE = 256
LANES = 128
STAGE_AT = (0, 10, 15, 21, 29, 37, 40, 52)
CHUNK_STEP = 8


def times_rows(left, right):
    return lax.dot_general(
        left, right, (((1,), (1,)), ((), ())), preferred_element_type=jnp.float32
    )


def columns_first(left, right):
    return lax.dot_general(
        left, right, (((0,), (0,)), ((), ())), preferred_element_type=jnp.float32
    )


def per_device(inputs, weight, enc_bias, dec_bias, row_code, lat_code, lat_thr, loss_scale):
    place = lax.axis_index("dat")
    lats = weight.shape[0]
    mine = lambda v: lax.dynamic_slice_in_dim(v, place * lats, lats, 0)
    rows = lax.all_gather(inputs, "dat", axis=0, tiled=True)
    total_rows = rows.shape[0]
    active = row_code[:, None] * mine(lat_code)[None, :] % 4093 < mine(lat_thr)[None, :]
    pre = (
        lax.psum(times_rows(rows, weight).astype(jnp.bfloat16), "wid").astype(jnp.float32)
        + mine(enc_bias)[None, :]
    )
    acts = jnp.where(active, pre, 0.0).astype(jnp.bfloat16)
    partial_value = jnp.dot(acts, weight, preferred_element_type=jnp.float32)
    recon = lax.psum(partial_value.astype(jnp.bfloat16), ("lat", "dat")).astype(jnp.float32)
    recon = recon + dec_bias[None, :]
    g_rec = loss_scale[0] * (2.0 / total_rows) * (recon - rows.astype(jnp.float32))
    g_bf = g_rec.astype(jnp.bfloat16)
    g_acts = lax.psum(times_rows(g_bf, weight).astype(jnp.bfloat16), "wid").astype(jnp.float32)
    g_pre = jnp.where(active, g_acts, 0.0).astype(jnp.bfloat16)
    grad_weight = (columns_first(acts, g_bf) + columns_first(g_pre, rows)).astype(jnp.bfloat16)
    latent_total = jnp.sum(g_pre.astype(jnp.float32), axis=0)
    grad_enc_bias = lax.all_gather(latent_total, "dat", axis=0, tiled=True)
    return (grad_weight, grad_enc_bias, jnp.sum(g_rec, axis=0))


def kernel(
    n_wid, n_lat, scale_ref, x_ref, w_ref, eb_ref, db_ref, rc_ref, lc_ref, thr_ref,
    gw_ref, ge_ref, gd_ref,
    x_all, p_out, p_in, acts_t, rec, rec_in, summed, near_in, paired, far_in, g_all, q_out, q_in, g_pre_t, grad, done, eb_sum,
    x_sem, p_sem, c_sem, s_sem, f_sem, a_sem, h_sem, q_sem, e_sem, w_sem,
):
    wid, lat, dat = lax.axis_index("wid"), lax.axis_index("lat"), lax.axis_index("dat")
    other = 1 - dat
    half, width = x_all.shape[2:]
    lats = w_ref.shape[0]
    rows = 2 * half
    wid_peers = [lax.rem(wid + k, n_wid) for k in range(1, n_wid)]
    side = lax.rem(lat, 2)
    near, far = lat + 1 - 2 * side, lax.rem(lat + 2, n_lat)

    barrier = pltpu.get_barrier_semaphore()
    everyone = [{"dat": other}] + [{"wid": p} for p in wid_peers] + [{"lat": near}, {"lat": far}]
    for peer in everyone:
        pl.semaphore_signal(barrier, inc=1, device_id=peer, device_id_type=MESH)
    pl.semaphore_wait(barrier, len(everyone))

    def copy(src, dst, sems, peer):
        return pltpu.make_async_remote_copy(
            src_ref=src, dst_ref=dst, send_sem=sems.at[0], recv_sem=sems.at[1],
            device_id=peer, device_id_type=MESH,
        )

    def x_copy(c):
        return copy(x_ref.at[c], x_all.at[c, dat], x_sem.at[c], {"dat": other})

    def p_copies(c):
        return [copy(p_out.at[c], p_in.at[c, k], p_sem.at[c, k], {"wid": p}) for k, p in enumerate(wid_peers)]

    def q_copies(c):
        return [copy(q_out.at[c], q_in.at[c, k], q_sem.at[c, k], {"wid": p}) for k, p in enumerate(wid_peers)]

    def c_copy(c):
        return copy(rec.at[c, other], rec_in.at[c], c_sem.at[c], {"dat": other})

    def s_copy(c):
        return copy(summed.at[c, 1 - side], near_in.at[c], s_sem.at[c], {"lat": near})

    def f_copy(c):
        return copy(paired.at[c], far_in.at[c], f_sem.at[c], {"lat": far})

    def a_copy(c):
        return copy(g_all.at[c, dat, side], g_all.at[c, dat, side], a_sem.at[c], {"lat": near})

    def h_copy(c):
        return copy(g_all.at[c, dat], g_all.at[c, dat], h_sem.at[c], {"dat": other})

    def row_codes(c):
        line = rc_ref[...].astype(F32)
        starts = (c * half, (CHUNKS + c) * half)
        line = jnp.concatenate([line[:, at:at + half] for at in starts], axis=1)
        return jnp.broadcast_to(line, (LANES, rows)).T[:, :1]

    def active(c):
        product = row_codes(c) * lc_ref[dat].astype(F32)
        left = product - jnp.floor(product * (1.0 / 4093.0)) * 4093.0
        left = jnp.where(left < 0.0, left + 4093.0, left)
        left = jnp.where(left >= 4093.0, left - 4093.0, left)
        return left < thr_ref[dat].astype(F32)

    def by_latents(value, out, c):
        for t in range(lats // TILE):
            cols = slice(t * TILE, (t + 1) * TILE)
            out[c, :, cols] = times_rows(value, w_ref[cols, :]).astype(BF16)

    def total(out, into, c):
        value = out[c].astype(F32)
        for k in range(n_wid - 1):
            value = value + into[c, k].astype(F32)
        return value

    def encode(c):
        x_copy(c).wait()
        by_latents(x_all[c].reshape(rows, width), p_out, c)
        for one in p_copies(c):
            one.start()

    def decode(c):
        for one in p_copies(c):
            one.wait()
        acts = jnp.where(active(c), total(p_out, p_in, c) + eb_ref[dat], 0.0)
        acts_t[:, c * rows:(c + 1) * rows] = acts.T.astype(BF16)
        acts = acts.astype(BF16)
        for t in range(width // TILE):
            cols = slice(t * TILE, (t + 1) * TILE)
            part = jnp.dot(acts, w_ref[:, cols], preferred_element_type=F32)
            rec[c, :, :, cols] = part.astype(BF16).reshape(2, half, TILE)
        c_copy(c).start()

    def core_sum(c):
        c_copy(c).wait()
        both = rec[c, dat].astype(F32) + rec_in[c].astype(F32)
        summed[c] = both.astype(BF16).reshape(summed.shape[1:])
        s_copy(c).start()

    def near_sum(c):
        s_copy(c).wait()
        paired[c] = (summed[c, side].astype(F32) + near_in[c].astype(F32)).astype(BF16)
        f_copy(c).start()

    def gradient(c):
        f_copy(c).wait()
        recon = paired[c].astype(F32) + far_in[c].astype(F32)
        own = x_piece(c)
        g_rec = scale_ref[0] * (2.0 / (rows * CHUNKS)) * (recon + bias_row() - own.astype(F32))
        g_all[c, dat, side] = g_rec.astype(BF16)
        a_copy(c).start()

    def bias_row():
        return jnp.concatenate([db_ref[i:i + 1, :] for i in range(width // LANES)], axis=1)

    def x_piece(c):
        count = half // 2
        return x_ref[c, pl.ds(pl.multiple_of(side * count, count), count), :]

    def share(c):
        a_copy(c).wait()
        h_copy(c).start()

    def back(c):
        h_copy(c).wait()
        g_rows = g_all[c].reshape(rows, width)
        column = jnp.sum(g_rows.astype(F32), axis=0, keepdims=True)
        for i in range(width // LANES):
            cell = column[:, i * LANES:(i + 1) * LANES]
            gd_ref[i:i + 1, :] = cell if c == 0 else gd_ref[i:i + 1, :] + cell
        by_latents(g_rows, q_out, c)
        for one in q_copies(c):
            one.start()

    def gate(c):
        for one in q_copies(c):
            one.wait()
        g_pre = jnp.where(active(c), total(q_out, q_in, c), 0.0).astype(BF16).astype(F32)
        g_pre_t[:, c * rows:(c + 1) * rows] = g_pre.T.astype(BF16)
        column = jnp.sum(g_pre, axis=0, keepdims=True)
        eb_sum[dat] = column if c == 0 else eb_sum[dat] + column

    def out_copy(t):
        cols = slice(t * TILE, (t + 1) * TILE)
        return pltpu.make_async_copy(done.at[:, cols], gw_ref.at[:, cols], w_sem.at[t])

    for c in range(CHUNKS):
        x_copy(c).start()
    x_all[:, dat] = x_ref[...]
    stages = (encode, decode, core_sum, near_sum, gradient, share, back, gate)
    order = sorted(
        (STAGE_AT[s] + (CHUNK_STEP if s else 1) * c, s, c) for s in range(len(stages)) for c in range(CHUNKS)
    )
    for _, s, c in order:
        if s == len(stages) - 1 and c == CHUNKS - 1:
            for t in range(width // TILE):
                cols = slice(t * TILE, (t + 1) * TILE)
                right = g_all[:, :, :, :, cols].reshape(CHUNKS * rows, TILE)
                early = x_all[:c, :, :, cols].reshape(c * rows, TILE)
                grad[:, cols] = jnp.dot(acts_t[...], right, preferred_element_type=F32) + jnp.dot(
                    g_pre_t[:, :c * rows], early, preferred_element_type=F32
                )
        stages[s](c)
    e_copy = copy(eb_sum.at[dat], eb_sum.at[dat], e_sem, {"dat": other})
    e_copy.start()
    for t in range(width // TILE):
        cols = slice(t * TILE, (t + 1) * TILE)
        right = x_all[CHUNKS - 1, :, :, cols].reshape(rows, TILE)
        late = jnp.dot(g_pre_t[:, (CHUNKS - 1) * rows:], right, preferred_element_type=F32)
        done[:, cols] = (grad[:, cols] + late).astype(BF16)
        out_copy(t).start()
    for t in range(width // TILE):
        out_copy(t).wait()
    e_copy.wait()
    ge_ref[...] = eb_sum[...]


def fused(n_wid, n_lat, inputs, weight, enc_bias, dec_bias, row_code, lat_code, lat_thr, loss_scale):
    lats, width = weight.shape
    half = inputs.shape[0] // CHUNKS
    rows, piece = 2 * half, half // 2
    whole = pl.BlockSpec(memory_space=pltpu.VMEM)
    pair = lambda v: v.reshape(2, 1, lats)
    sems = lambda *shape: pltpu.SemaphoreType.DMA(shape + (2,))
    grad_weight, grad_enc_bias, grad_dec_bias = pl.pallas_call(
        functools.partial(kernel, n_wid, n_lat),
        out_shape=(
            jax.ShapeDtypeStruct((lats, width), BF16),
            jax.ShapeDtypeStruct((2, 1, lats), F32),
            jax.ShapeDtypeStruct((width // LANES, LANES), F32),
        ),
        in_specs=[pl.BlockSpec(memory_space=pltpu.SMEM)] + [whole] * 7,
        out_specs=(pl.BlockSpec(memory_space=pl.ANY), whole, whole),
        scratch_shapes=[
            pltpu.VMEM((CHUNKS, 2, half, width), BF16),
            pltpu.VMEM((CHUNKS, rows, lats), BF16),
            pltpu.VMEM((CHUNKS, n_wid - 1, rows, lats), BF16),
            pltpu.VMEM((lats, CHUNKS * rows), BF16),
            pltpu.VMEM((CHUNKS, 2, half, width), BF16),
            pltpu.VMEM((CHUNKS, half, width), BF16),
            pltpu.VMEM((CHUNKS, 2, piece, width), BF16),
            pltpu.VMEM((CHUNKS, piece, width), BF16),
            pltpu.VMEM((CHUNKS, piece, width), BF16),
            pltpu.VMEM((CHUNKS, piece, width), BF16),
            pltpu.VMEM((CHUNKS, 2, 2, piece, width), BF16),
            pltpu.VMEM((CHUNKS, rows, lats), BF16),
            pltpu.VMEM((CHUNKS, n_wid - 1, rows, lats), BF16),
            pltpu.VMEM((lats, CHUNKS * rows), BF16),
            pltpu.VMEM((lats, width), F32),
            pltpu.VMEM((lats, width), BF16),
            pltpu.VMEM((2, 1, lats), F32),
            sems(CHUNKS), sems(CHUNKS, n_wid - 1), sems(CHUNKS), sems(CHUNKS),
            sems(CHUNKS), sems(CHUNKS), sems(CHUNKS), sems(CHUNKS, n_wid - 1), sems(),
            pltpu.SemaphoreType.DMA((width // TILE,)),
        ],
        compiler_params=pltpu.CompilerParams(
            collective_id=0, has_side_effects=True, vmem_limit_bytes=56 * 1024 * 1024
        ),
    )(
        loss_scale, inputs.reshape(CHUNKS, half, width), weight, pair(enc_bias),
        dec_bias.reshape(width // LANES, LANES), row_code.reshape(1, -1), pair(lat_code), pair(lat_thr),
    )
    return (grad_weight, grad_enc_bias.reshape(-1), grad_dec_bias.reshape(-1))


def fits(mesh, rows, lats, width):
    n_wid, n_lat = mesh.shape["wid"], mesh.shape["lat"]
    return (
        mesh.shape["dat"] == 2 and n_wid == 2 and n_lat == 4
        and rows % (CHUNKS * 2 * 16) == 0 and lats % TILE == 0 and 2 * rows % (CHUNKS * LANES) == 0 and width % TILE == 0
        and lats * width <= 2 ** 21 and rows <= 256
    )


def solution(mesh):
    def body(inputs, weight, *rest):
        if fits(mesh, inputs.shape[0], weight.shape[0], weight.shape[1]):
            return fused(mesh.shape["wid"], mesh.shape["lat"], inputs, weight, *rest)
        return per_device(inputs, weight, *rest)

    return jax.shard_map(
        body,
        mesh=mesh,
        in_specs=(
            P(("groups", "dat"), "wid"),
            P(("groups", "lat", "dat"), "wid"),
            P(("groups", "lat")),
            P(("groups", "wid")),
            P("groups"),
            P(("groups", "lat")),
            P(("groups", "lat")),
            P(),
        ),
        out_specs=(P(("groups", "lat", "dat"), "wid"), P(("groups", "lat")), P(("groups", "wid"))),
        check_vma=False,
    )
```
